32 devices in a mesh: req: 8 (over z, x), head: 2 (over y), side: 2 (over core).
Axes of the slice: x: 2, y: 2, z: 4, core: 2. Of those that a mesh axis runs over, the one named last changes fastest.
Arguments:
- query: bfloat16 [64, 128, 128], P(('req', 'side'), 'head'), may hold values from -40 to 40
- keys: bfloat16 [64, 8, 192, 128], P(('req', 'side'), 'head'), may hold values from -40 to 40
- values: bfloat16 [64, 8, 192, 128], P(('req', 'side'), 'head'), may hold values from -12 to 12
- lengths: int32 [64], P(('req', 'side')), may hold values from 2 to 192, as said below
- residual: bfloat16 [64, 16384], P(None, ('req', 'side')), may hold values from -6 to 6
- out_weight: bfloat16 [16384, 16384], P('head', ('req', 'side')), may hold values from -0.046875 to 0.046875
- norm_gain: float32 [16384], P(('req', 'side')), may hold values from 0.5 to 1.5
- gate_weight: bfloat16 [16384, 26624], P(('req', 'side'), 'head'), may hold values from -0.046875 to 0.046875
- up_weight: bfloat16 [16384, 26624], P(('req', 'side'), 'head'), may hold values from -0.046875 to 0.046875
- down_weight: bfloat16 [26624, 16384], P('head', ('req', 'side')), may hold values from -0.0390625 to 0.0390625
Outputs:
- output: bfloat16 [64, 16384], P('head', ('req', 'side'))
The draws below stay inside these ranges and needn't reach their ends.
Inputs may be any that keep to these rules, and one draw needn't show every extreme that they name: `lengths`: the first request of each block of 4 requests has length 192.
All inputs are finite; a program needn't handle non-finite values.
Results may differ from the reference program's by a relative error of at most 0.0048.
Values may be sent and summed in bfloat16 or wider, within the bound.
A program may use at most 192 MiB of HBM per device.

```python
import math
import jax
import jax.numpy as jnp
from jax import lax

D = 16384
H = 128
KVH = 8
HD = 128
FF = 26624
REQ_DEV = 4
LMAX = 192
REQS = 64


def shared_normal(key):
    return jax.random.normal(key, (REQS, KVH, LMAX, HD), jnp.float32)


def draw_keys(key, part):
    base = shared_normal(key)
    return jnp.clip(base, -40.0, 40.0).astype(jnp.bfloat16)


def draw_query(key, part):
    anchor = key
    key = jax.random.fold_in(anchor, 5)
    own_draw = jax.random.normal(key, (REQS, H, HD), jnp.float32)
    return jnp.clip(own_draw, -40.0, 40.0).astype(jnp.bfloat16)


def draw_lengths(key, part):
    key = jax.random.fold_in(key, 9)
    drawn = jax.random.randint(key, (REQS,), 2, LMAX + 1)
    return jnp.where(jnp.arange(REQS) % REQ_DEV == 0, LMAX, drawn).astype(jnp.int32)


def shard_levels(rng, dims, shards, smallest, top_value):
    def one(dim, shards_of):
        heights = jax.random.uniform(jax.random.fold_in(jax.random.fold_in(rng, 6), dim), (shards_of,), jnp.float32, smallest / len(shards), top_value / len(shards))
        return jnp.repeat(jnp.exp(heights), dims[dim] // shards_of).reshape((-1,) + (1,) * (len(dims) - dim - 1))

    gain = one(*shards[0])
    for cut in shards[1:]:
        gain = gain * one(*cut)
    return gain


def centred(own_key, extent, width, reach, split=(), kind=jnp.bfloat16):
    result = jax.random.normal(own_key, extent, jnp.float32) * width
    if len(split) > 0:
        result = shard_levels(own_key, extent, split, -0.22, 0.18) * result
    return jnp.clip(result, min=-reach, max=reach).astype(kind)


def setup_inputs(seed: int = 0) -> dict:
    arg_keys = jax.random.split(jax.random.key(seed), 11)
    query = draw_query(jax.random.fold_in(arg_keys[10], 71), 0)
    keys = draw_keys(jax.random.fold_in(arg_keys[10], 71), 0)
    values = centred(arg_keys[2], (REQS, KVH, LMAX, HD), 2.0, 12.0, ((0, 16), (1, 2)))
    lengths = draw_lengths(jax.random.fold_in(arg_keys[10], 71), 0)
    residual = centred(arg_keys[4], (REQS, D), 1.0, 6.0, ((1, 16),))
    out_weight = centred(arg_keys[5], (H * HD, D), (H * HD) ** -0.5, 0.046875, ((0, 2), (1, 16)))
    norm_gain = jnp.clip(1.0 + 0.1 * jax.random.normal(arg_keys[6], (D,), jnp.float32), 0.5, 1.5)
    gate_weight = centred(arg_keys[7], (D, FF), D ** -0.5, 0.046875, ((0, 16), (1, 2)))
    up_weight = centred(arg_keys[8], (D, FF), D ** -0.5, 0.046875, ((0, 16), (1, 2)))
    down_weight = centred(arg_keys[9], (FF, D), FF ** -0.5, 0.0390625, ((0, 2), (1, 16)))
    return dict(query=query, keys=keys, values=values, lengths=lengths, residual=residual, out_weight=out_weight, norm_gain=norm_gain, gate_weight=gate_weight, up_weight=up_weight, down_weight=down_weight)


def reference(query, keys, values, lengths, residual, out_weight, norm_gain, gate_weight, up_weight, down_weight):
    group_size = H // KVH
    grouped = query.reshape(REQS, KVH, group_size, HD).astype(jnp.float32)
    scores = jnp.einsum('rkgd,rkpd->rkgp', grouped, keys.astype(jnp.float32)) / math.sqrt(HD)
    positions = jnp.arange(LMAX, dtype=jnp.int32)
    usable = positions[None, :] < lengths[:, None]
    scores = jnp.where(usable[:, None, None, :], scores, -1e+30)
    row_max = lax.optimization_barrier(jnp.max(scores, axis=-1, keepdims=True))
    weights = jnp.exp(scores - row_max)
    weight_sum = lax.optimization_barrier(jnp.sum(weights, axis=-1, keepdims=True))
    rounded = lax.optimization_barrier(weights.astype(jnp.bfloat16))
    context = jnp.einsum('rkgp,rkpd->rkgd', rounded.astype(jnp.float32), values.astype(jnp.float32))
    attended = (context / weight_sum).reshape(REQS, H * HD).astype(jnp.bfloat16)
    projected = jnp.dot(attended, out_weight, preferred_element_type=jnp.float32)
    stream = residual.astype(jnp.float32) + projected
    squares = lax.optimization_barrier(jnp.sum(stream * stream, axis=1))
    scaled = (stream * lax.rsqrt(squares[:, None] / D + 1e-05) * norm_gain).astype(jnp.bfloat16)
    gate = jnp.dot(scaled, gate_weight, preferred_element_type=jnp.float32)
    upward = jnp.dot(scaled, up_weight, preferred_element_type=jnp.float32)
    hidden = (jax.nn.silu(gate) * upward).astype(jnp.bfloat16)
    lowered = jnp.dot(hidden, down_weight, preferred_element_type=jnp.float32)
    return (stream + lowered).astype(jnp.bfloat16)
```

```python
import functools
import math

import jax
import jax.numpy as jnp
from jax import lax
from jax.experimental import pallas as pl
from jax.experimental.pallas import tpu as pltpu
from jax.sharding import PartitionSpec as P

MESH = pl.DeviceIdType.MESH
F32 = jnp.float32
BF16 = jnp.bfloat16


def low_bit(k):
    return (k & -k).bit_length() - 1


def flip(index, k):
    out = index
    b = 0
    while (1 << b) <= k:
        if k & (1 << b):
            bit = lax.rem(lax.div(index, jnp.int32(1 << b)), jnp.int32(2))
            out = out + (1 - 2 * bit) * (1 << b)
        b += 1
    return out


def tiles(width, step):
    return [(s, min(step, width - s)) for s in range(0, width, step)]


def layer_kernel(
    n_req, quarters, d_model,
    att_ref, res_ref, gain_ref, ow_hbm, gate_hbm, up_hbm, down_hbm,
    out_ref,
    ow, down2, gu, ag, xq, stream, xs, psend, precv, sqsend, sqrecv,
    acc, s_send, s_recv, t_send, t_recv, hid, low, low_send, low_recv,
    ow_sem, gu_sem, down_sem,
    ag_ss, ag_rs, agc_ss, agc_rs,
    p_ss, p_rs, sq_ss, sq_rs,
    sc_ss, sc_rs, t_ss, t_rs,
    h_ss, h_rs, hc_ss, hc_rs, l_ss, l_rs,
):
    bits = n_req.bit_length() - 1
    me = lax.axis_index("req")
    head = lax.axis_index("head")
    side = lax.axis_index("side")
    rows, width = stream.shape
    half = rows // 2
    chunk = acc.shape[-1]
    k_part = xq.shape[-1]
    in_ow = ow.shape[0] // chunk
    gu_slots = gu.shape[0]

    def req_peer(b):
        return (flip(me, 1 << b), head, side)

    sibling = (me, head, 1 - side)
    across = (me, 1 - head, side)

    def ow_copy(q):
        part = pl.ds(q * k_part, k_part)
        return pltpu.make_async_copy(ow_hbm.at[part], ow.at[part], ow_sem.at[q])

    def gu_copies(k):
        columns = pl.ds(pl.multiple_of(flip(me, k) * chunk, 128), chunk)
        slot = (n_req - 1 - k) % gu_slots
        return [
            pltpu.make_async_copy(hbm.at[:, columns], gu.at[slot, j], gu_sem.at[slot, j])
            for j, hbm in enumerate((gate_hbm, up_hbm))
        ]

    def down_place(k):
        if k < in_ow:
            return ow.at[pl.ds(k * chunk, chunk)]
        return down2.at[k - in_ow]

    def down_copy(k):
        part = pl.ds(pl.multiple_of(flip(me, k) * chunk, 128), chunk)
        return pltpu.make_async_copy(down_hbm.at[part], down_place(k), down_sem.at[k])

    for q in range(quarters):
        ow_copy(q).start()
    for k in range(n_req - 1, n_req - 1 - gu_slots, -1):
        for c in gu_copies(k):
            c.start()
    for k in range(in_ow, n_req):
        down_copy(k).start()

    barrier = pltpu.get_barrier_semaphore()
    peers = [sibling, across] + [req_peer(b) for b in range(bits)]
    for peer in peers:
        pl.semaphore_signal(barrier, inc=1, device_id=peer, device_id_type=MESH)
    pl.semaphore_wait(barrier, len(peers))

    def remote(src, dst, ss, rs, peer):
        return pltpu.make_async_remote_copy(
            src_ref=src, dst_ref=dst, send_sem=ss, recv_sem=rs, device_id=peer, device_id_type=MESH
        )

    def ag_tree(m):
        b = low_bit(m)
        block = ag.at[flip(me, m ^ (1 << b)), side]
        return remote(block, block, ag_ss.at[m], ag_rs.at[m], req_peer(b))

    def ag_tree_arrival(m):
        block = ag.at[flip(me, m), side]
        return remote(block, block, ag_ss.at[m], ag_rs.at[m], req_peer(low_bit(m)))

    def ag_core(k):
        block = ag.at[flip(me, k), side]
        return remote(block, block, agc_ss.at[k], agc_rs.at[k], sibling)

    def ag_core_arrival(k):
        block = ag.at[flip(me, k), 1 - side]
        return remote(block, block, agc_ss.at[k], agc_rs.at[k], sibling)

    def hid_tree(m):
        b = low_bit(m)
        return remote(
            hid.at[m ^ (1 << b), 0], hid.at[m, 0], h_ss.at[m], h_rs.at[m], req_peer(b)
        )

    def hid_core(k):
        return remote(hid.at[k, 0], hid.at[k, 1], hc_ss.at[k], hc_rs.at[k], sibling)

    def forward(k, tree, core):
        top = bits if k == 0 else low_bit(k)
        for b in range(top - 1, -1, -1):
            tree(k | (1 << b)).start()
        core(k).start()

    arrival = sorted(range(1, n_req), key=lambda k: (bin(k).count("1"), -low_bit(k)))

    ag[me, side] = att_ref[...]
    forward(0, ag_tree, ag_core)
    for k in arrival:
        ag_tree_arrival(k).wait_recv()
        forward(k, ag_tree, ag_core)
    for k in range(n_req):
        ag_core_arrival(k).wait_recv()

    local = rows // (2 * n_req)
    per = ag.shape[2]
    total_rows = 2 * n_req * per
    request = lax.broadcasted_iota(jnp.int32, (rows, total_rows), 0)
    held = lax.broadcasted_iota(jnp.int32, (rows, total_rows), 1)
    for q in range(quarters):
        wanted = (request // local) * per + q * local + request % local
        pick = jnp.where(held == wanted, 1.0, 0.0).astype(BF16)
        for s, w in tiles(k_part, 512):
            gathered = ag[:, :, :, s : s + w].reshape(total_rows, w)
            xq[q, :, s : s + w] = jnp.dot(pick, gathered, preferred_element_type=F32).astype(BF16)

    halves = psend.shape[0]
    wide = width // halves

    def p_copy(n):
        return remote(psend.at[n], precv.at[n], p_ss.at[n], p_rs.at[n], across)

    for n in range(halves):
        cols = slice(n * wide, (n + 1) * wide)
        total = None
        for q in range(quarters):
            if n == 0:
                ow_copy(q).wait()
            part = jnp.dot(
                xq[q], ow[q * k_part : (q + 1) * k_part, cols], preferred_element_type=F32
            )
            total = part if total is None else total + part
        psend[n] = total.astype(BF16)
        p_copy(n).start()
        stream[:, cols] = total + res_ref[:, cols].astype(F32)
    for n in range(halves):
        cols = slice(n * wide, (n + 1) * wide)
        p_copy(n).wait_recv()
        stream[:, cols] = stream[:, cols] + precv[n].astype(F32)

    own = pl.ds(pl.multiple_of(side * half, half), half)
    other = pl.ds(pl.multiple_of((1 - side) * half, half), half)
    xs[0:half, :] = (stream[own, :] * gain_ref[...]).astype(BF16)
    xs[half:rows, :] = (stream[other, :] * gain_ref[...]).astype(BF16)
    value = stream[...]
    sqsend[0] = jnp.broadcast_to(jnp.sum(value * value, axis=1, keepdims=True), (rows, 128))

    def sq_copy(b):
        peer = sibling if b == 0 else req_peer(b - 1)
        return remote(sqsend.at[b], sqrecv.at[b], sq_ss.at[b], sq_rs.at[b], peer)

    sq_copy(0).start()

    def sq_step(b):
        sq_copy(b).wait_recv()
        sqsend[b + 1] = sqsend[b] + sqrecv[b]
        if b < bits:
            sq_copy(b + 1).start()

    def core_copy(k):
        return remote(s_send.at[k], s_recv.at[k], sc_ss.at[k], sc_rs.at[k], sibling)

    def tree_copy(k):
        return remote(t_send.at[k], t_recv.at[k], t_ss.at[k], t_rs.at[k], req_peer(low_bit(k)))

    def compute(k):
        slot = (n_req - 1 - k) % gu_slots
        for j, c in enumerate(gu_copies(k)):
            c.wait()
            for s, w in tiles(chunk, 512):
                y = jnp.dot(xs[...], gu[slot, j, :, s : s + w], preferred_element_type=F32)
                acc[k, j, :, s : s + w] = y[0:half]
                s_send[k, j, :, s : s + w] = y[half:rows].astype(BF16)
        core_copy(k).start()
        if k - gu_slots >= 0:
            for c in gu_copies(k - gu_slots):
                c.start()

    def core_done(k):
        core_copy(k).wait_recv()
        if k % 2 == 1:
            t_send[k] = (acc[k] + s_recv[k].astype(F32)).astype(BF16)
            tree_copy(k).start()
        else:
            acc[k] = acc[k] + s_recv[k].astype(F32)

    def summed(k, j, s, w):
        out = acc[k, j, :, s : s + w]
        for b in range(bits if k == 0 else low_bit(k)):
            out = out + t_recv[k | (1 << b), j, :, s : s + w].astype(F32)
        return out

    def tree_wait(k):
        for b in range(bits if k == 0 else low_bit(k)):
            tree_copy(k | (1 << b)).wait_recv()

    def pass_on(k):
        tree_wait(k)
        for j in range(2):
            for s, w in tiles(chunk, 512):
                t_send[k, j, :, s : s + w] = summed(k, j, s, w).astype(BF16)
        tree_copy(k).start()

    for step, k in enumerate(range(n_req - 1, -1, -1)):
        compute(k)
        if step < in_ow and step < n_req:
            down_copy(step).start()
        if k + 1 < n_req:
            core_done(k + 1)
        late = k + 3
        if late < n_req and late % 2 == 0 and late > 0:
            pass_on(late)
        if step <= bits:
            sq_step(step)
    core_done(0)
    if n_req > 2:
        pass_on(2)
    tree_wait(0)

    scale = lax.rsqrt(sqsend[bits + 1, own, 0:1] / d_model + 1e-05)
    for s, w in tiles(chunk, 512):
        gate = summed(0, 0, s, w) * scale
        up = summed(0, 1, s, w) * scale
        hid[0, 0, :, s : s + w] = (gate / (1.0 + jnp.exp(-gate)) * up).astype(BF16)

    forward(0, hid_tree, hid_core)

    def lower(k, first):
        hid_core(k).wait_recv()
        down_copy(k).wait()
        place = down_place(k)
        x = hid[k].reshape(rows, chunk)
        for s, w in tiles(width, 512):
            y = jnp.dot(x, place[:, s : s + w], preferred_element_type=F32)
            if first:
                low[:, s : s + w] = y
            else:
                low[:, s : s + w] = low[:, s : s + w] + y

    pending = [0]
    for k in arrival:
        hid_tree(k).wait_recv()
        forward(k, hid_tree, hid_core)
        if len(pending) > 2 or k == arrival[0]:
            j = pending.pop(0)
            lower(j, j == 0)
        pending.append(k)
    for j in pending:
        lower(j, j == 0)

    mine = pl.ds(pl.multiple_of(lax.rem(head + side, 2) * half, half), half)
    theirs = pl.ds(pl.multiple_of(lax.rem(head + side + 1, 2) * half, half), half)
    low_send[...] = low[theirs, :]
    last = remote(low_send, low_recv, l_ss.at[0], l_rs.at[0], across)
    last.start()
    kept = stream[pl.ds(pl.multiple_of(head * half, half), half), :] + low[mine, :]
    last.wait_recv()
    out_ref[...] = (kept + low_recv[...]).astype(out_ref.dtype)

    last.wait_send()
    for n in range(halves):
        p_copy(n).wait_send()
    for b in range(bits + 1):
        sq_copy(b).wait_send()
    for k in range(n_req):
        ag_core(k).wait_send()
        core_copy(k).wait_send()
        hid_core(k).wait_send()
        if k > 0:
            ag_tree(k).wait_send()
            tree_copy(k).wait_send()
            hid_tree(k).wait_send()


def layer(att, residual, norm_gain, out_weight, gate_weight, up_weight, down_weight, n_req, d_model):
    rows, width = residual.shape
    per, k_part = att.shape
    k_local = out_weight.shape[0]
    quarters = k_local // k_part
    ff = gate_weight.shape[1]
    chunk = ff // n_req
    half = rows // 2
    bits = n_req.bit_length() - 1
    in_ow = min(n_req, -(-k_local // chunk))
    gu_slots = min(2, n_req)
    dma = lambda *shape: pltpu.SemaphoreType.DMA(shape)
    vmem = lambda shape, dtype: pltpu.VMEM(shape, dtype)
    piece = (n_req, 2, half, chunk)
    scratch = [
        vmem((max(in_ow * chunk, k_local), width), BF16),
        vmem((max(n_req - in_ow, 1), chunk, width), BF16),
        vmem((gu_slots, 2, width, chunk), BF16),
        vmem((n_req, 2, per, k_part), BF16),
        vmem((quarters, rows, k_part), BF16),
        vmem((rows, width), F32),
        vmem((rows, width), BF16),
        vmem((2, rows, width // 2), BF16),
        vmem((2, rows, width // 2), BF16),
        vmem((bits + 2, rows, 128), F32),
        vmem((bits + 1, rows, 128), F32),
        vmem(piece, F32),
        vmem(piece, BF16),
        vmem(piece, BF16),
        vmem(piece, BF16),
        vmem(piece, BF16),
        vmem(piece, BF16),
        vmem((rows, width), F32),
        vmem((half, width), F32),
        vmem((half, width), F32),
        dma(quarters), dma(gu_slots, 2), dma(n_req),
        dma(n_req), dma(n_req), dma(n_req), dma(n_req),
        dma(2), dma(2), dma(bits + 1), dma(bits + 1),
        dma(n_req), dma(n_req), dma(n_req), dma(n_req),
        dma(n_req), dma(n_req), dma(n_req), dma(n_req), dma(1), dma(1),
    ]
    in_vmem = pl.BlockSpec(memory_space=pltpu.VMEM)
    anywhere = pl.BlockSpec(memory_space=pl.ANY)
    weights = k_local * width + 2 * width * ff + ff * width
    return pl.pallas_call(
        functools.partial(layer_kernel, n_req, quarters, d_model),
        out_shape=jax.ShapeDtypeStruct((half, width), BF16),
        in_specs=[in_vmem] * 3 + [anywhere] * 4,
        out_specs=in_vmem,
        scratch_shapes=scratch,
        compiler_params=pltpu.CompilerParams(
            collective_id=0, has_side_effects=True, vmem_limit_bytes=60 * 1024 * 1024
        ),
        cost_estimate=pl.CostEstimate(
            flops=2 * rows * weights, bytes_accessed=2 * weights, transcendentals=0
        ),
    )(att, residual, norm_gain.reshape(1, width), out_weight, gate_weight, up_weight, down_weight)


def attention(query, keys, values, lengths):
    local_reqs, local_heads, head_dim = query.shape
    local_kv = keys.shape[1]
    cache_len = keys.shape[2]
    group_size = local_heads // local_kv
    grouped = query.reshape(local_reqs, local_kv, group_size, head_dim)
    scores = jnp.einsum(
        "rkgd,rkpd->rkgp", grouped, keys, preferred_element_type=F32
    ) / math.sqrt(head_dim)
    positions = jnp.arange(cache_len, dtype=jnp.int32)
    usable = positions[None, :] < lengths[:, None]
    scores = jnp.where(usable[:, None, None, :], scores, -1e30)
    row_max = jnp.max(scores, axis=-1, keepdims=True)
    weights = jnp.exp(scores - row_max)
    weight_sum = jnp.sum(weights, axis=-1, keepdims=True)
    context = jnp.einsum(
        "rkgp,rkpd->rkgd", weights.astype(BF16), values, preferred_element_type=F32
    )
    return (context / weight_sum).reshape(local_reqs, local_heads * head_dim).astype(BF16)


def plain_shards(
    d_model, query, keys, values, lengths, residual, out_weight, norm_gain, gate_weight, up_weight, down_weight
):
    attended = attention(query, keys, values, lengths)
    head_part = jnp.dot(
        lax.all_gather(attended, ("req", "side"), axis=0, tiled=True),
        out_weight,
        preferred_element_type=F32,
    )
    projected = lax.psum(head_part, "head")
    stream = residual.astype(F32) + projected
    squares = lax.psum(jnp.sum(stream * stream, axis=1), ("req", "side"))
    scaled = (stream * lax.rsqrt(squares[:, None] / d_model + 1e-05) * norm_gain).astype(BF16)
    gate_sum, up_sum = lax.psum(
        (
            jnp.dot(scaled, gate_weight, preferred_element_type=F32),
            jnp.dot(scaled, up_weight, preferred_element_type=F32),
        ),
        ("req", "side"),
    )
    hidden = (jax.nn.silu(gate_sum) * up_sum).astype(BF16)
    lowered = jnp.dot(hidden, down_weight, preferred_element_type=F32)
    reduced = lax.psum_scatter(lowered, "head", scatter_dimension=0, tiled=True)
    row_count = reduced.shape[0]
    own_rows = lax.dynamic_slice_in_dim(stream, lax.axis_index("head") * row_count, row_count, 0)
    return (own_rows + reduced).astype(BF16)


def fused_shards(
    n_req, d_model, query, keys, values, lengths, residual, out_weight, norm_gain, gate_weight, up_weight, down_weight
):
    attended = attention(query, keys, values, lengths)
    local_reqs, k_local = attended.shape
    quarters = 16 // local_reqs
    block = attended.reshape(local_reqs, quarters, k_local // quarters)
    block = block.transpose(1, 0, 2).reshape(16, k_local // quarters)
    return layer(block, residual, norm_gain, out_weight, gate_weight, up_weight, down_weight, n_req, d_model)


def solution(mesh):
    n_req, n_head, n_side = mesh.shape["req"], mesh.shape["head"], mesh.shape["side"]

    def shards(query, keys, values, lengths, residual, out_weight, norm_gain, gate_weight, up_weight, down_weight):
        rows, width = residual.shape
        local_reqs = query.shape[0]
        d_model = width * n_req * n_side
        ff = gate_weight.shape[1]
        fits = (
            n_side == 2
            and n_head == 2
            and n_req >= 4
            and n_req & (n_req - 1) == 0
            and ff % (n_req * 128) == 0
            and rows % 32 == 0
            and 16 % local_reqs == 0
            and out_weight.shape[0] % ((16 // local_reqs) * 128) == 0
        )
        body = functools.partial(fused_shards, n_req, d_model) if fits else functools.partial(plain_shards, d_model)
        return body(query, keys, values, lengths, residual, out_weight, norm_gain, gate_weight, up_weight, down_weight)

    in_specs = (
        P(("req", "side"), "head", None),
        P(("req", "side"), "head", None, None),
        P(("req", "side"), "head", None, None),
        P(("req", "side")),
        P(None, ("req", "side")),
        P("head", ("req", "side")),
        P(("req", "side")),
        P(("req", "side"), "head"),
        P(("req", "side"), "head"),
        P("head", ("req", "side")),
    )
    out_specs = P("head", ("req", "side"))
    return jax.shard_map(shards, mesh=mesh, in_specs=in_specs, out_specs=out_specs, check_vma=False)
```

```python
import functools
import math

import jax
import jax.numpy as jnp
from jax import lax
from jax.experimental import pallas as pl
from jax.experimental.pallas import tpu as pltpu
from jax.sharding import PartitionSpec as P

MESH = pl.DeviceIdType.MESH
F32 = jnp.float32
BF16 = jnp.bfloat16


def low_bit(k):
    return (k & -k).bit_length() - 1


def flip(index, k):
    out = index
    b = 0
    while (1 << b) <= k:
        if k & (1 << b):
            bit = lax.rem(lax.div(index, jnp.int32(1 << b)), jnp.int32(2))
            out = out + (1 - 2 * bit) * (1 << b)
        b += 1
    return out


def tiles(width, step):
    return [(s, min(step, width - s)) for s in range(0, width, step)]


def layer_kernel(
    n_req, quarters, d_model,
    len_ref, query_ref, key_ref, value_ref, res_ref, gain_ref, ow_hbm, gate_hbm, up_hbm, down_hbm,
    out_ref,
    ctx, ow, down2, gu, ag, xq, stream, xs, psend, precv, sqsend, sqrecv,
    acc, s_send, s_recv, t_send, t_recv, hid, low, low_send, low_recv,
    ow_sem, gu_sem, down_sem,
    ag_ss, ag_rs, agc_ss, agc_rs,
    p_ss, p_rs, sq_ss, sq_rs,
    sc_ss, sc_rs, t_ss, t_rs,
    h_ss, h_rs, hc_ss, hc_rs, l_ss, l_rs,
):
    bits = n_req.bit_length() - 1
    me = lax.axis_index("req")
    head = lax.axis_index("head")
    side = lax.axis_index("side")
    rows, width = stream.shape
    half = rows // 2
    chunk = acc.shape[-1]
    k_part = xq.shape[-1]
    in_ow = ow.shape[0] // chunk
    gu_slots = gu.shape[0]

    def req_peer(b):
        return (flip(me, 1 << b), head, side)

    sibling = (me, head, 1 - side)
    across = (me, 1 - head, side)

    def ow_copy(q):
        part = pl.ds(q * k_part, k_part)
        return pltpu.make_async_copy(ow_hbm.at[part], ow.at[part], ow_sem.at[q])

    def gu_copies(k):
        columns = pl.ds(pl.multiple_of(flip(me, k) * chunk, 128), chunk)
        slot = (n_req - 1 - k) % gu_slots
        return [
            pltpu.make_async_copy(hbm.at[:, columns], gu.at[slot, j], gu_sem.at[slot, j])
            for j, hbm in enumerate((gate_hbm, up_hbm))
        ]

    def down_place(k):
        if k < in_ow:
            return ow.at[pl.ds(k * chunk, chunk)]
        return down2.at[k - in_ow]

    def down_copy(k):
        part = pl.ds(pl.multiple_of(flip(me, k) * chunk, 128), chunk)
        return pltpu.make_async_copy(down_hbm.at[part], down_place(k), down_sem.at[k])

    for q in range(quarters):
        ow_copy(q).start()
    for k in range(n_req - 1, n_req - 1 - gu_slots, -1):
        for c in gu_copies(k):
            c.start()
    for k in range(in_ow, n_req):
        down_copy(k).start()

    barrier = pltpu.get_barrier_semaphore()
    peers = [sibling, across] + [req_peer(b) for b in range(bits)]
    for peer in peers:
        pl.semaphore_signal(barrier, inc=1, device_id=peer, device_id_type=MESH)

    local_reqs, local_kv, cache_len, head_dim = key_ref.shape
    group = query_ref.shape[1] // local_kv
    positions = lax.broadcasted_iota(jnp.int32, (group, cache_len), 1)
    for g in range(local_kv):
        for r in range(local_reqs):
            scores = lax.dot_general(
                query_ref[r, g * group : (g + 1) * group, :], key_ref[r, g],
                (((1,), (1,)), ((), ())), preferred_element_type=F32,
            ) / math.sqrt(head_dim)
            scores = jnp.where(positions < len_ref[r], scores, -1e30)
            weights = jnp.exp(scores - jnp.max(scores, axis=1, keepdims=True))
            weight_sum = jnp.sum(weights, axis=1, keepdims=True)
            context = jnp.dot(weights.astype(BF16), value_ref[r, g], preferred_element_type=F32)
            ctx[g * local_reqs + r] = context / weight_sum
    for h in range(group):
        ag[me, side, :, h * head_dim : (h + 1) * head_dim] = ctx[:, h, :].astype(BF16)

    pl.semaphore_wait(barrier, len(peers))

    def remote(src, dst, ss, rs, peer):
        return pltpu.make_async_remote_copy(
            src_ref=src, dst_ref=dst, send_sem=ss, recv_sem=rs, device_id=peer, device_id_type=MESH
        )

    def ag_tree(m):
        b = low_bit(m)
        block = ag.at[flip(me, m ^ (1 << b)), side]
        return remote(block, block, ag_ss.at[m], ag_rs.at[m], req_peer(b))

    def ag_tree_arrival(m):
        block = ag.at[flip(me, m), side]
        return remote(block, block, ag_ss.at[m], ag_rs.at[m], req_peer(low_bit(m)))

    def ag_core(k):
        block = ag.at[flip(me, k), side]
        return remote(block, block, agc_ss.at[k], agc_rs.at[k], sibling)

    def ag_core_arrival(k):
        block = ag.at[flip(me, k), 1 - side]
        return remote(block, block, agc_ss.at[k], agc_rs.at[k], sibling)

    def hid_tree(m):
        b = low_bit(m)
        return remote(
            hid.at[m ^ (1 << b), 0], hid.at[m, 0], h_ss.at[m], h_rs.at[m], req_peer(b)
        )

    def hid_core(k):
        return remote(hid.at[k, 0], hid.at[k, 1], hc_ss.at[k], hc_rs.at[k], sibling)

    def forward(k, tree, core):
        top = bits if k == 0 else low_bit(k)
        for b in range(top - 1, -1, -1):
            tree(k | (1 << b)).start()
        core(k).start()

    arrival = sorted(
        range(1, n_req),
        key=lambda k: (bin(k).count("1"), low_bit(k) if k & (k - 1) == 0 else -low_bit(k)),
    )

    forward(0, ag_tree, ag_core)
    for k in arrival:
        ag_tree_arrival(k).wait_recv()
        forward(k, ag_tree, ag_core)
    for k in range(n_req):
        ag_core_arrival(k).wait_recv()

    local = rows // (2 * n_req)
    per = ag.shape[2]
    total_rows = 2 * n_req * per
    request = lax.broadcasted_iota(jnp.int32, (rows, total_rows), 0)
    held = lax.broadcasted_iota(jnp.int32, (rows, total_rows), 1)
    for q in range(quarters):
        wanted = (request // local) * per + q * local + request % local
        pick = jnp.where(held == wanted, 1.0, 0.0).astype(BF16)
        for s, w in tiles(k_part, 512):
            gathered = ag[:, :, :, s : s + w].reshape(total_rows, w)
            xq[q, :, s : s + w] = jnp.dot(pick, gathered, preferred_element_type=F32).astype(BF16)

    halves = psend.shape[0]
    wide = width // halves

    def p_copy(n):
        return remote(psend.at[n], precv.at[n], p_ss.at[n], p_rs.at[n], across)

    for n in range(halves):
        cols = slice(n * wide, (n + 1) * wide)
        total = None
        for q in range(quarters):
            if n == 0:
                ow_copy(q).wait()
            part = jnp.dot(
                xq[q], ow[q * k_part : (q + 1) * k_part, cols], preferred_element_type=F32
            )
            total = part if total is None else total + part
        psend[n] = total.astype(BF16)
        p_copy(n).start()
        stream[:, cols] = total + res_ref[:, cols].astype(F32)
    for n in range(halves):
        cols = slice(n * wide, (n + 1) * wide)
        p_copy(n).wait_recv()
        stream[:, cols] = stream[:, cols] + precv[n].astype(F32)

    own = pl.ds(pl.multiple_of(side * half, half), half)
    other = pl.ds(pl.multiple_of((1 - side) * half, half), half)
    xs[0:half, :] = (stream[own, :] * gain_ref[...]).astype(BF16)
    xs[half:rows, :] = (stream[other, :] * gain_ref[...]).astype(BF16)
    value = stream[...]
    sqsend[0] = jnp.broadcast_to(jnp.sum(value * value, axis=1, keepdims=True), (rows, 128))

    def sq_copy(b):
        peer = sibling if b == 0 else req_peer(b - 1)
        return remote(sqsend.at[b], sqrecv.at[b], sq_ss.at[b], sq_rs.at[b], peer)

    sq_copy(0).start()

    def sq_step(b):
        sq_copy(b).wait_recv()
        sqsend[b + 1] = sqsend[b] + sqrecv[b]
        if b < bits:
            sq_copy(b + 1).start()

    def core_copy(k):
        return remote(s_send.at[k], s_recv.at[k], sc_ss.at[k], sc_rs.at[k], sibling)

    def tree_copy(k):
        return remote(t_send.at[k], t_recv.at[k], t_ss.at[k], t_rs.at[k], req_peer(low_bit(k)))

    def compute(k):
        slot = (n_req - 1 - k) % gu_slots
        for j, c in enumerate(gu_copies(k)):
            c.wait()
            for s, w in tiles(chunk, 512):
                y = jnp.dot(xs[...], gu[slot, j, :, s : s + w], preferred_element_type=F32)
                acc[k, j, :, s : s + w] = y[0:half]
                s_send[k, j, :, s : s + w] = y[half:rows]
        core_copy(k).start()
        if k - gu_slots >= 0:
            for c in gu_copies(k - gu_slots):
                c.start()

    def core_done(k):
        core_copy(k).wait_recv()
        if k % 2 == 1:
            t_send[k] = (acc[k] + s_recv[k]).astype(BF16)
            tree_copy(k).start()
        else:
            acc[k] = acc[k] + s_recv[k]

    def summed(k, j, s, w):
        out = acc[k, j, :, s : s + w]
        for b in range(bits if k == 0 else low_bit(k)):
            out = out + t_recv[k | (1 << b), j, :, s : s + w].astype(F32)
        return out

    def tree_wait(k):
        for b in range(bits if k == 0 else low_bit(k)):
            tree_copy(k | (1 << b)).wait_recv()

    def pass_on(k):
        tree_wait(k)
        for j in range(2):
            for s, w in tiles(chunk, 512):
                t_send[k, j, :, s : s + w] = summed(k, j, s, w).astype(BF16)
        tree_copy(k).start()

    for step, k in enumerate(range(n_req - 1, -1, -1)):
        compute(k)
        if step < in_ow and step < n_req:
            down_copy(step).start()
        if k + 1 < n_req:
            core_done(k + 1)
        late = k + 3
        if late < n_req and late % 2 == 0 and late > 0:
            pass_on(late)
        if step <= bits:
            sq_step(step)
    core_done(0)
    if n_req > 2:
        pass_on(2)
    tree_wait(0)

    scale = lax.rsqrt(sqsend[bits + 1, own, 0:1] / d_model + 1e-05)
    for s, w in tiles(chunk, 512):
        gate = summed(0, 0, s, w) * scale
        up = summed(0, 1, s, w) * scale
        hid[0, 0, :, s : s + w] = (gate / (1.0 + jnp.exp(-gate)) * up).astype(BF16)

    forward(0, hid_tree, hid_core)

    def lower(k, first):
        hid_core(k).wait_recv()
        down_copy(k).wait()
        place = down_place(k)
        x = hid[k].reshape(rows, chunk)
        for s, w in tiles(width, 512):
            y = jnp.dot(x, place[:, s : s + w], preferred_element_type=F32)
            if first:
                low[:, s : s + w] = y
            else:
                low[:, s : s + w] = low[:, s : s + w] + y

    pending = [0]
    for k in arrival:
        while k == arrival[-1] and pending:
            j = pending.pop(0)
            lower(j, j == 0)
        hid_tree(k).wait_recv()
        forward(k, hid_tree, hid_core)
        if len(pending) > 1:
            j = pending.pop(0)
            lower(j, j == 0)
        pending.append(k)
    for j in pending:
        lower(j, j == 0)

    mine = pl.ds(pl.multiple_of(lax.rem(head + side, 2) * half, half), half)
    theirs = pl.ds(pl.multiple_of(lax.rem(head + side + 1, 2) * half, half), half)
    low_send[...] = low[theirs, :]
    last = remote(low_send, low_recv, l_ss.at[0], l_rs.at[0], across)
    last.start()
    kept = stream[pl.ds(pl.multiple_of(head * half, half), half), :] + low[mine, :]
    last.wait_recv()
    out_ref[...] = (kept + low_recv[...]).astype(out_ref.dtype)

    last.wait_send()
    for n in range(halves):
        p_copy(n).wait_send()
    for b in range(bits + 1):
        sq_copy(b).wait_send()
    for k in range(n_req):
        ag_core(k).wait_send()
        core_copy(k).wait_send()
        hid_core(k).wait_send()
        if k > 0:
            ag_tree(k).wait_send()
            tree_copy(k).wait_send()
            hid_tree(k).wait_send()


def layer(query, keys, values, lengths, residual, norm_gain, out_weight, gate_weight, up_weight, down_weight, n_req, d_model):
    rows, width = residual.shape
    local_reqs, local_kv, _, head_dim = keys.shape
    group = query.shape[1] // local_kv
    k_local = out_weight.shape[0]
    quarters = local_kv
    per, k_part = quarters * local_reqs, k_local // quarters
    ff = gate_weight.shape[1]
    chunk = ff // n_req
    half = rows // 2
    bits = n_req.bit_length() - 1
    in_ow = min(n_req, -(-k_local // chunk))
    gu_slots = min(2, n_req)
    dma = lambda *shape: pltpu.SemaphoreType.DMA(shape)
    vmem = lambda shape, dtype: pltpu.VMEM(shape, dtype)
    piece = (n_req, 2, half, chunk)
    scratch = [
        vmem((per, group, head_dim), F32),
        vmem((max(in_ow * chunk, k_local), width), BF16),
        vmem((max(n_req - in_ow, 1), chunk, width), BF16),
        vmem((gu_slots, 2, width, chunk), BF16),
        vmem((n_req, 2, per, k_part), BF16),
        vmem((quarters, rows, k_part), BF16),
        vmem((rows, width), F32),
        vmem((rows, width), BF16),
        vmem((2, rows, width // 2), BF16),
        vmem((2, rows, width // 2), BF16),
        vmem((bits + 2, rows, 128), F32),
        vmem((bits + 1, rows, 128), F32),
        vmem(piece, F32),
        vmem(piece, F32),
        vmem(piece, F32),
        vmem(piece, BF16),
        vmem(piece, BF16),
        vmem(piece, BF16),
        vmem((rows, width), F32),
        vmem((half, width), F32),
        vmem((half, width), F32),
        dma(quarters), dma(gu_slots, 2), dma(n_req),
        dma(n_req), dma(n_req), dma(n_req), dma(n_req),
        dma(2), dma(2), dma(bits + 1), dma(bits + 1),
        dma(n_req), dma(n_req), dma(n_req), dma(n_req),
        dma(n_req), dma(n_req), dma(n_req), dma(n_req), dma(1), dma(1),
    ]
    in_vmem = pl.BlockSpec(memory_space=pltpu.VMEM)
    anywhere = pl.BlockSpec(memory_space=pl.ANY)
    weights = k_local * width + 2 * width * ff + ff * width
    return pl.pallas_call(
        functools.partial(layer_kernel, n_req, quarters, d_model),
        out_shape=jax.ShapeDtypeStruct((half, width), BF16),
        in_specs=[pl.BlockSpec(memory_space=pltpu.SMEM)] + [in_vmem] * 5 + [anywhere] * 4,
        out_specs=in_vmem,
        scratch_shapes=scratch,
        compiler_params=pltpu.CompilerParams(
            collective_id=0, has_side_effects=True, vmem_limit_bytes=62 * 1024 * 1024
        ),
        cost_estimate=pl.CostEstimate(
            flops=2 * rows * weights, bytes_accessed=2 * weights, transcendentals=0
        ),
    )(
        lengths, query, keys, values, residual, norm_gain.reshape(1, width),
        out_weight, gate_weight, up_weight, down_weight,
    )


def attention(query, keys, values, lengths):
    local_reqs, local_heads, head_dim = query.shape
    local_kv = keys.shape[1]
    cache_len = keys.shape[2]
    group_size = local_heads // local_kv
    grouped = query.reshape(local_reqs, local_kv, group_size, head_dim)
    scores = jnp.einsum(
        "rkgd,rkpd->rkgp", grouped, keys, preferred_element_type=F32
    ) / math.sqrt(head_dim)
    positions = jnp.arange(cache_len, dtype=jnp.int32)
    usable = positions[None, :] < lengths[:, None]
    scores = jnp.where(usable[:, None, None, :], scores, -1e30)
    row_max = jnp.max(scores, axis=-1, keepdims=True)
    weights = jnp.exp(scores - row_max)
    weight_sum = jnp.sum(weights, axis=-1, keepdims=True)
    context = jnp.einsum(
        "rkgp,rkpd->rkgd", weights.astype(BF16), values, preferred_element_type=F32
    )
    return (context / weight_sum).reshape(local_reqs, local_heads * head_dim).astype(BF16)


def plain_shards(
    d_model, query, keys, values, lengths, residual, out_weight, norm_gain, gate_weight, up_weight, down_weight
):
    attended = attention(query, keys, values, lengths)
    head_part = jnp.dot(
        lax.all_gather(attended, ("req", "side"), axis=0, tiled=True),
        out_weight,
        preferred_element_type=F32,
    )
    projected = lax.psum(head_part, "head")
    stream = residual.astype(F32) + projected
    squares = lax.psum(jnp.sum(stream * stream, axis=1), ("req", "side"))
    scaled = (stream * lax.rsqrt(squares[:, None] / d_model + 1e-05) * norm_gain).astype(BF16)
    gate_sum, up_sum = lax.psum(
        (
            jnp.dot(scaled, gate_weight, preferred_element_type=F32),
            jnp.dot(scaled, up_weight, preferred_element_type=F32),
        ),
        ("req", "side"),
    )
    hidden = (jax.nn.silu(gate_sum) * up_sum).astype(BF16)
    lowered = jnp.dot(hidden, down_weight, preferred_element_type=F32)
    reduced = lax.psum_scatter(lowered, "head", scatter_dimension=0, tiled=True)
    row_count = reduced.shape[0]
    own_rows = lax.dynamic_slice_in_dim(stream, lax.axis_index("head") * row_count, row_count, 0)
    return (own_rows + reduced).astype(BF16)


def fused_shards(
    n_req, d_model, query, keys, values, lengths, residual, out_weight, norm_gain, gate_weight, up_weight, down_weight
):
    return layer(
        query, keys, values, lengths, residual, norm_gain,
        out_weight, gate_weight, up_weight, down_weight, n_req, d_model,
    )


def solution(mesh):
    n_req, n_head, n_side = mesh.shape["req"], mesh.shape["head"], mesh.shape["side"]

    def shards(query, keys, values, lengths, residual, out_weight, norm_gain, gate_weight, up_weight, down_weight):
        rows, width = residual.shape
        local_reqs = query.shape[0]
        d_model = width * n_req * n_side
        ff = gate_weight.shape[1]
        fits = (
            n_side == 2
            and n_head == 2
            and n_req >= 4
            and n_req & (n_req - 1) == 0
            and ff % (n_req * 128) == 0
            and rows % 32 == 0
            and local_reqs * keys.shape[1] == 16
            and query.shape[2] % 128 == 0
        )
        body = functools.partial(fused_shards, n_req, d_model) if fits else functools.partial(plain_shards, d_model)
        return body(query, keys, values, lengths, residual, out_weight, norm_gain, gate_weight, up_weight, down_weight)

    in_specs = (
        P(("req", "side"), "head", None),
        P(("req", "side"), "head", None, None),
        P(("req", "side"), "head", None, None),
        P(("req", "side")),
        P(None, ("req", "side")),
        P("head", ("req", "side")),
        P(("req", "side")),
        P(("req", "side"), "head"),
        P(("req", "side"), "head"),
        P("head", ("req", "side")),
    )
    out_specs = P("head", ("req", "side"))
    return jax.shard_map(shards, mesh=mesh, in_specs=in_specs, out_specs=out_specs, check_vma=False)
```
